256 devices in a mesh: section: 8 (over z_hi, y), dp: 32 (over z_lo, x, core).
Axes of the slice: x: 4, y: 4, z: 8 (z_hi: 2, z_lo: 4; z = z_hi * 4 + z_lo), core: 2. Of those that a mesh axis runs over, the one named last changes fastest.
Arguments:
- inputs: bfloat16 [2, 4096, 2048], P(None, 'dp'), may hold values from -6 to 6
- cotangent: bfloat16 [2, 4096, 2048], P(None, 'dp'), may hold values from -6 to 6
- weights: bfloat16 [8, 2048, 2048], P('section'), may hold values from -0.125 to 0.125
- gains: float32 [8, 2048], P('section'), may hold values from 0.1 to 1.9
Outputs:
- grad_input: bfloat16 [8, 2, 4096, 2048], P('section', None, 'dp')
- weight_grad: float32 [8, 2048, 2048], P('section', 'dp')
- gain_grad: float32 [8, 2048], P('section')
The draws below stay inside these ranges and needn't reach their ends.
All inputs are finite; a program needn't handle non-finite values.
Results may differ from the reference program's by a relative error of at most 0.033.
Values may be sent and summed in bfloat16 or wider, within the bound.
A program may use at most 128 MiB of HBM per device.

```python
import math
import jax
import jax.numpy as jnp
from jax import lax

D = 2048
MB = 2
SECTIONS = 8
TOKENS = 4096


def with_spikes(drawn, key, source, target, shards_of, factor):
    owner, partner = [(jnp.arange(drawn.shape[dim]) // (drawn.shape[dim] // shards_of)).reshape([-1 if axis == dim else 1 for axis in range(drawn.ndim)]) for dim in (source, target)]
    chosen = jax.random.permutation(key, shards_of)[partner]
    strong = (owner == chosen) | (owner == (partner + shards_of // 2) % shards_of)
    return jnp.where(strong, factor * drawn, drawn)


def levels(rng, shape, shards, low, top_value):
    level, own = 1.0, jax.random.fold_in(rng, 6)
    for dim, shards_of in shards:
        steps = jnp.exp(jax.random.uniform(jax.random.fold_in(own, dim), (shards_of,), jnp.float32, low / len(shards), top_value / len(shards)))
        level = level * jnp.repeat(steps, shape[dim] // shards_of).reshape([-1 if axis == dim else 1 for axis in range(len(shape))])
    return level


def gaussian(rng, dims, scale, reach, shards=(), dtype=jnp.bfloat16):
    array = scale * jax.random.normal(rng, dims, jnp.float32)
    if shards:
        array = array * levels(rng, dims, shards, -0.22, 0.18)
    return jnp.clip(array, -reach, reach).astype(dtype)


def noise_with(own_key, extent, scale, bound, split, heavy, kind=jnp.bfloat16):
    values = scale * jax.random.normal(own_key, extent, jnp.float32)
    if split:
        values = values * levels(own_key, extent, split, -0.22, 0.18)
    return jnp.clip(with_spikes(values, jax.random.fold_in(own_key, 3), *heavy), -bound, bound).astype(kind)


def setup_inputs(seed: int = 0) -> dict:
    seeds = jax.random.split(jax.random.key(seed), 5)
    inputs = noise_with(seeds[0], (MB, TOKENS, D), 1.0, 6.0, ((1, 32),), (1, 2, 32, 2.75))
    cotangent = gaussian(seeds[1], (MB, TOKENS, D), 1.0, 6.0, ((1, 32),))
    weights = gaussian(seeds[2], (SECTIONS, D, D), D ** -0.5, 0.125, ((0, 8),))
    gains = jnp.clip(1.0 + 0.18 * jax.random.normal(seeds[3], (SECTIONS, D), jnp.float32), 0.1, 1.9)
    return dict(inputs=inputs, cotangent=cotangent, weights=weights, gains=gains)


eps = 1e-05

def normalize(act, gain):
    af = act.astype(jnp.float32)
    radius = jnp.sqrt(lax.optimization_barrier(jnp.mean(af * af, axis=-1, keepdims=True)) + eps)
    normed = (af / radius * gain).astype(jnp.bfloat16)
    return (af, radius, normed)

def reference(inputs, cotangent, weights, gains):
    width = inputs.shape[-1]
    act = inputs.reshape(-1, width)
    stored = []
    for layer in range(SECTIONS):
        stored.append(act)
        af, radius, normed = normalize(act, gains[layer])
        act = (af + jnp.dot(normed, weights[layer], preferred_element_type=jnp.float32)).astype(jnp.bfloat16)
    scale = 1.0 / math.sqrt(MB * TOKENS)
    upstream = cotangent.reshape(-1, width)
    grads_in = []
    grads_w = []
    grads_g = []
    for layer in range(SECTIONS - 1, -1, -1):
        af, radius, normed = normalize(stored[layer], gains[layer])
        dnorm = lax.dot_general(upstream, weights[layer], (((1,), (1,)), ((), ())), preferred_element_type=jnp.float32)
        wterm = lax.dot_general(normed, upstream, (((0,), (0,)), ((), ())), preferred_element_type=jnp.float32)
        grads_w.insert(0, wterm * scale)
        grads_g.insert(0, lax.optimization_barrier(jnp.sum(dnorm * af / radius, axis=0)) * scale)
        gdn = gains[layer] * dnorm
        back = upstream.astype(jnp.float32) + gdn / radius - af * lax.optimization_barrier(jnp.sum(gdn * af, axis=-1, keepdims=True)) / (width * radius ** 3)
        upstream = back.astype(jnp.bfloat16)
        grads_in.insert(0, upstream.reshape(inputs.shape))
    return (jnp.stack(grads_in), jnp.stack(grads_w), jnp.stack(grads_g))
```

```python
import functools
import math

import jax
import jax.numpy as jnp
from jax import lax
from jax.experimental import pallas as pl
from jax.experimental.pallas import tpu as pltpu
from jax.sharding import PartitionSpec as P

eps = 1e-05
MESH = pl.DeviceIdType.MESH
NX = 4
CHUNK = 16
PIECES = 4
bf16 = jnp.bfloat16
f32 = jnp.float32


def kernel(
    n_section, n_dp, scale,
    inputs, cotangent, weights, gains,
    grad_in, w_out, g_out,
    w, wt, act, act_out, gath, n_send, n_gath, rinv, acc, dw,
    core_send, core_recv, z_send, z_recv, gacc, g_send, gx_recv, gc_send, gc_recv, gz_send, gz_recv,
    load_sem, w_sem, fs_sem, fr_sem, bs_sem, br_sem, xs_sem, xr_sem, ns_sem, nr_sem,
    cs_sem, cr_sem, zs_sem, zr_sem, gs_sem, gr_sem,
):
    rows, width = act.shape
    steps = rows // CHUNK
    kw = width // PIECES
    nz = n_dp // (2 * NX)
    zw = width // nz
    xw = zw // NX
    cw = xw // 2
    s = lax.axis_index("section")
    d = lax.axis_index("dp")
    core = d % 2
    x = (d // 2) % NX
    z = d // (2 * NX)
    first, last = s == 0, s == n_section - 1

    def at_x(j):
        return {"section": s, "dp": (z * NX + (x + j) % NX) * 2 + core}

    def at_z(j):
        return {"section": s, "dp": (((z + j) % nz) * NX + x) * 2 + core}

    partner = {"section": s, "dp": d + 1 - 2 * core}
    above = {"section": (s + 1) % n_section, "dp": d}
    below = {"section": (s + n_section - 1) % n_section, "dp": d}

    def remote(src, dst, send, recv, to):
        return pltpu.make_async_remote_copy(
            src_ref=src, dst_ref=dst, send_sem=send, recv_sem=recv, device_id=to, device_id_type=MESH
        )

    def w_load(k):
        part = pl.ds(k * kw, kw)
        return pltpu.make_async_copy(weights.at[part], w.at[part], w_sem.at[k])

    load_act = pltpu.make_async_copy(inputs, act, load_sem.at[0])
    load_cot = pltpu.make_async_copy(cotangent, gath.at[0], load_sem.at[1])

    @pl.when(first)
    def _():
        load_act.start()

    for k in range(PIECES):
        w_load(k).start()

    @pl.when(last)
    def _():
        load_cot.start()

    gacc[...] = jnp.zeros_like(gacc)

    barrier = pltpu.get_barrier_semaphore()
    peers = [at_x(j) for j in range(1, NX)] + [at_z(j) for j in range(1, nz)] + [partner, above, below]
    for to in peers:
        pl.semaphore_signal(barrier, inc=1, device_id=to, device_id_type=MESH)
    pl.semaphore_wait(barrier, len(peers))

    @pl.when(first)
    def _():
        load_act.wait()

    @pl.when(last)
    def _():
        load_cot.wait()

    def up(i, k):
        part = (pl.ds(pl.multiple_of(i * CHUNK, CHUNK), CHUNK), pl.ds(k * kw, kw))
        return remote(act_out.at[part], act.at[part], fs_sem.at[0], fr_sem.at[i, k], above)

    def down(i, k):
        part = (pl.ds(pl.multiple_of(i * CHUNK, CHUNK), CHUNK), pl.ds(k * kw, kw))
        return remote(grad_in.at[part], gath.at[0].at[part], bs_sem.at[0], br_sem.at[i, k], below)

    def gather(i, j):
        part = pl.ds(pl.multiple_of(i * CHUNK, CHUNK), CHUNK)
        return remote(
            gath.at[0, part], gath.at[NX - j, part], xs_sem.at[j - 1], xr_sem.at[NX - j - 1], at_x(j)
        )

    def gather_all(j):
        return remote(gath.at[0], gath.at[NX - j], xs_sem.at[j - 1], xr_sem.at[NX - j - 1], at_x(j))

    def n_gather(j):
        return remote(
            n_send.at[j - 1], n_gath.at[NX - j], ns_sem.at[j - 1], nr_sem.at[NX - j - 1], at_x(j)
        )

    def forward(i):
        part = pl.ds(pl.multiple_of(i * CHUNK, CHUNK), CHUNK)
        square = jnp.zeros((CHUNK, 1), f32)
        for k in range(PIECES):
            cols = pl.ds(k * kw, kw)

            @pl.when(jnp.logical_not(first))
            def _():
                up(i, k).wait_recv()

            a = act[part, cols].astype(f32)
            square = square + jnp.sum(a * a, axis=-1, keepdims=True)

            @pl.when(i == 0)
            def _():
                @pl.when(first)
                def _():
                    w_load(k).wait()

            @pl.when(jnp.logical_not(last))
            def _():
                b = (act[part, cols].astype(f32) * gains[:, cols]).astype(bf16)
                term = jnp.dot(b, w[cols, :], preferred_element_type=f32)
                if k == 0:
                    acc[...] = term
                else:
                    acc[...] += term

        inv = 1.0 / jnp.sqrt(square / width + eps)
        rinv[part, :] = jnp.broadcast_to(inv, (CHUNK, 128))

        @pl.when(jnp.logical_not(last))
        def _():
            for k in range(PIECES):
                cols = pl.ds(k * kw, kw)
                act_out[part, cols] = (
                    act[part, cols].astype(f32) + acc[:, k * kw : (k + 1) * kw] * inv
                ).astype(bf16)
                up(i, k).start()

        for j in range(NX):
            xj = (x + j) % NX
            for zi in range(nz):
                cols = pl.ds(pl.multiple_of(zi * zw + xj * xw, xw), xw)
                v = (act[part, cols].astype(f32) * inv * gains[:, cols]).astype(bf16)
                if j == 0:
                    n_gath[0, part, zi * xw : (zi + 1) * xw] = v
                else:
                    n_send[j - 1, part, zi * xw : (zi + 1) * xw] = v

        @pl.when(i == steps - 1)
        def _():
            for j in range(1, NX):
                n_gather(j).start()

    def backward(i):
        part = pl.ds(pl.multiple_of(i * CHUNK, CHUNK), CHUNK)
        for k in range(PIECES):
            cols = pl.ds(k * kw, kw)

            @pl.when(jnp.logical_not(last))
            def _():
                down(i, k).wait_recv()

            term = jnp.dot(gath[0, part, cols], wt[cols, :], preferred_element_type=f32)
            if k == 0:
                acc[...] = term
            else:
                acc[...] += term
        inv = rinv[part, 0:1]
        along = jnp.zeros((CHUNK, 1), f32)
        for k in range(PIECES):
            cols = slice(k * kw, (k + 1) * kw)
            along = along + jnp.sum(
                acc[:, cols] * gains[:, cols] * act[part, cols].astype(f32), axis=-1, keepdims=True
            )
        back = along * (inv * inv * inv) / width
        for k in range(PIECES):
            cols = slice(k * kw, (k + 1) * kw)
            af = act[part, cols].astype(f32)
            dn = acc[:, cols]
            grad_in[part, cols] = (
                gath[0, part, cols].astype(f32) + gains[:, cols] * dn * inv - af * back
            ).astype(bf16)

            @pl.when(jnp.logical_not(first))
            def _():
                down(i, k).start()

        for j in range(1, NX):
            gather(i, j).start()
        for k in range(PIECES):
            cols = slice(k * kw, (k + 1) * kw)
            v = acc[:, cols] * act[part, cols].astype(f32) * inv
            total = v[0:8]
            for q in range(8, CHUNK, 8):
                total = total + v[q : q + 8]
            gacc[:, cols] += total

    lead = jnp.clip(2 * (2 * (n_section - 1 - s) + 1), 1, steps)

    def step(t, carry):
        @pl.when(((t == 0) & jnp.logical_not(first)) | ((t == steps) & first))
        def _():
            @pl.when(jnp.logical_not(first))
            def _():
                for k in range(PIECES):
                    w_load(k).wait()

            side = min(256, width)
            tiles = width // side

            def flip(q, c):
                at = pl.ds(pl.multiple_of(q // tiles * side, side), side)
                to = pl.ds(pl.multiple_of(q % tiles * side, side), side)
                wt[to, at] = w[at, to].T
                return c

            lax.fori_loop(0, tiles * tiles, flip, 0)

        @pl.when(t < steps)
        def _():
            forward(t)

        @pl.when((t >= lead) & (t - lead < steps))
        def _():
            backward(t - lead)

        return carry

    lax.fori_loop(0, 2 * steps, step, 0)

    def gain_x(j):
        return remote(g_send, gx_recv.at[NX - j - 1], gs_sem.at[j - 1], gr_sem.at[NX - j - 1], at_x(j))

    def gain_z(j):
        return remote(
            gz_send, gz_recv.at[nz - j - 1], gs_sem.at[NX + j - 1], gr_sem.at[NX + nz - j - 1], at_z(j)
        )

    gain_core = remote(gc_send, gc_recv, gs_sem.at[NX - 1], gr_sem.at[NX - 1], partner)

    g_send[...] = jnp.sum(gacc[...], axis=0, keepdims=True)
    for j in range(1, NX):
        gain_x(j).start()

    for j in range(1, NX):
        gather_all(j).wait()
        n_gather(j).wait()

    def core_swap(zj):
        return remote(core_send.at[zj], core_recv.at[zj], cs_sem.at[zj], cr_sem.at[zj], partner)

    def z_swap(j):
        return remote(
            z_send.at[j - 1], z_recv.at[nz - j - 1], zs_sem.at[j - 1], zr_sem.at[nz - j - 1], at_z(j)
        )

    mine = pl.ds(pl.multiple_of(core * cw, cw), cw)
    other = pl.ds(pl.multiple_of((1 - core) * cw, cw), cw)
    order = list(range(nz - 1, 0, -1)) + [0]
    for j in order:
        zj = (z + j) % nz
        cols = pl.ds(pl.multiple_of(zj * xw, xw), xw)
        for half in range(2):
            span = slice(half * (width // 2), (half + 1) * (width // 2))
            total = None
            for q in range(NX):
                term = lax.dot_general(
                    n_gath[q, :, cols], gath[q, :, span], (((0,), (0,)), ((), ())),
                    preferred_element_type=f32,
                )
                total = term if total is None else total + term
            dw[j, :, span] = total
        core_send[j] = dw[j, other, :].astype(bf16)
        core_swap(j).start()

    for j in range(1, NX):
        gain_x(j).wait()
    total = g_send[...]
    for j in range(1, NX):
        total = total + gx_recv[j - 1]
    gc_send[...] = total
    gain_core.start()

    for j in order:
        core_swap(j).wait()
        if j:
            z_send[j - 1] = (dw[j, mine, :] + core_recv[j].astype(f32)).astype(bf16)
            z_swap(j).start()

    gain_core.wait()
    gz_send[...] = gc_send[...] + gc_recv[...]
    for j in range(1, nz):
        gain_z(j).start()

    total = dw[0, mine, :] + core_recv[0].astype(f32)
    for j in range(1, nz):
        z_swap(j).wait()
        total = total + z_recv[nz - j - 1].astype(f32)
    w_out[...] = total * scale

    total = gz_send[...]
    for j in range(1, nz):
        gain_z(j).wait()
        total = total + gz_recv[nz - j - 1]
    g_out[...] = total * scale

    @pl.when(jnp.logical_not(last))
    def _():
        remote(act_out, act, fs_sem.at[0], fr_sem.at[0, 0], above).wait_send()

    @pl.when(jnp.logical_not(first))
    def _():
        remote(grad_in, gath.at[0], bs_sem.at[0], br_sem.at[0, 0], below).wait_send()


def on_device(n_section, n_dp, inputs, cotangent, weights, gains):
    micro, tok_rows, width = inputs.shape
    rows = micro * tok_rows
    nz = n_dp // (2 * NX)
    steps = rows // CHUNK
    xw = width // nz // NX
    cw = xw // 2
    scale = 1.0 / math.sqrt(rows * n_dp)
    vmem, dma = pltpu.VMEM, pltpu.SemaphoreType.DMA
    grad_in, w_out, g_out = pl.pallas_call(
        functools.partial(kernel, n_section, n_dp, scale),
        out_shape=(
            jax.ShapeDtypeStruct((rows, width), bf16),
            jax.ShapeDtypeStruct((cw, width), f32),
            jax.ShapeDtypeStruct((1, width), f32),
        ),
        in_specs=[pl.BlockSpec(memory_space=pl.ANY)] * 3 + [pl.BlockSpec(memory_space=vmem)],
        out_specs=[pl.BlockSpec(memory_space=vmem)] * 3,
        scratch_shapes=[
            vmem((width, width), bf16),
            vmem((width, width), bf16),
            vmem((rows, width), bf16),
            vmem((rows, width), bf16),
            vmem((NX, rows, width), bf16),
            vmem((NX - 1, rows, nz * xw), bf16),
            vmem((NX, rows, nz * xw), bf16),
            vmem((rows, 128), f32),
            vmem((CHUNK, width), f32),
            vmem((nz, xw, width), f32),
            vmem((nz, cw, width), bf16),
            vmem((nz, cw, width), bf16),
            vmem((nz - 1, cw, width), bf16),
            vmem((nz - 1, cw, width), bf16),
            vmem((8, width), f32),
            vmem((1, width), f32),
            vmem((NX - 1, 1, width), f32),
            vmem((1, width), f32),
            vmem((1, width), f32),
            vmem((1, width), f32),
            vmem((nz - 1, 1, width), f32),
            dma((2,)),
            dma((PIECES,)),
            dma((1,)),
            dma((steps, PIECES)),
            dma((1,)),
            dma((steps, PIECES)),
            dma((NX - 1,)),
            dma((NX - 1,)),
            dma((NX - 1,)),
            dma((NX - 1,)),
            dma((nz,)),
            dma((nz,)),
            dma((nz - 1,)),
            dma((nz - 1,)),
            dma((NX + nz - 1,)),
            dma((NX + nz - 1,)),
        ],
        compiler_params=pltpu.CompilerParams(
            collective_id=0, has_side_effects=True, vmem_limit_bytes=56 * 1024 * 1024
        ),
        name="relay",
    )(inputs.reshape(rows, width), cotangent.reshape(rows, width), weights[0], gains)
    return grad_in.reshape(1, micro, tok_rows, width), w_out[None], g_out


def solution(mesh):
    return jax.shard_map(
        functools.partial(on_device, mesh.shape["section"], mesh.shape["dp"]),
        mesh=mesh,
        in_specs=(
            P(None, "dp", None),
            P(None, "dp", None),
            P("section", None, None),
            P("section", None),
        ),
        out_specs=(P("section", None, "dp", None), P("section", "dp", None), P("section", None)),
        check_vma=False,
    )
```

```python
import functools
import math

import jax
import jax.numpy as jnp
from jax import lax
from jax.experimental import pallas as pl
from jax.experimental.pallas import tpu as pltpu
from jax.sharding import PartitionSpec as P

eps = 1e-05
MESH = pl.DeviceIdType.MESH
NX = 4
CHUNK = 16
PIECES_UP = 2
PIECES = 4
GROUPS = 4
BEHIND = 2
AHEAD = 3
bf16 = jnp.bfloat16
f32 = jnp.float32


def kernel(
    n_section, n_dp, scale,
    inputs, cotangent, weights, gains,
    grad_in, w_out, g_out,
    w, wt, act, act_out, gath, n_send, n_gath, rinv, acc, dw,
    core_send, core_recv, z_send, z_recv, gacc, g_send, gx_recv, gc_send, gc_recv, gz_send, gz_recv,
    load_sem, w_sem, fs_sem, fr_sem, bs_sem, br_sem, xs_sem, xr_sem, ns_sem, nr_sem,
    cs_sem, cr_sem, zs_sem, zr_sem, gs_sem, gr_sem,
):
    rows, width = act.shape
    steps = rows // CHUNK
    kw = width // PIECES
    nz = n_dp // (2 * NX)
    zw = width // nz
    xw = zw // NX
    cw = xw // 2
    s = lax.axis_index("section")
    d = lax.axis_index("dp")
    core = d % 2
    x = (d // 2) % NX
    z = d // (2 * NX)
    first, last = s == 0, s == n_section - 1

    def at_x(j):
        return {"section": s, "dp": (z * NX + (x + j) % NX) * 2 + core}

    def at_z(j):
        return {"section": s, "dp": (((z + j) % nz) * NX + x) * 2 + core}

    partner = {"section": s, "dp": d + 1 - 2 * core}
    above = {"section": (s + 1) % n_section, "dp": d}
    below = {"section": (s + n_section - 1) % n_section, "dp": d}

    def remote(src, dst, send, recv, to):
        return pltpu.make_async_remote_copy(
            src_ref=src, dst_ref=dst, send_sem=send, recv_sem=recv, device_id=to, device_id_type=MESH
        )

    def w_load(k):
        part = pl.ds(k * kw, kw)
        return pltpu.make_async_copy(weights.at[part], w.at[part], w_sem.at[k])

    load_act = pltpu.make_async_copy(inputs, act, load_sem.at[0])
    load_cot = pltpu.make_async_copy(cotangent, gath.at[0], load_sem.at[1])

    @pl.when(first)
    def _():
        load_act.start()

    for k in range(PIECES):
        w_load(k).start()

    @pl.when(last)
    def _():
        load_cot.start()

    gacc[...] = jnp.zeros_like(gacc)

    barrier = pltpu.get_barrier_semaphore()
    peers = [at_x(j) for j in range(1, NX)] + [at_z(j) for j in range(1, nz)] + [partner, above, below]
    for to in peers:
        pl.semaphore_signal(barrier, inc=1, device_id=to, device_id_type=MESH)
    pl.semaphore_wait(barrier, len(peers))

    @pl.when(first)
    def _():
        load_act.wait()

    @pl.when(last)
    def _():
        load_cot.wait()

    kf = width // PIECES_UP

    def up(i, k):
        part = (pl.ds(pl.multiple_of(i * CHUNK, CHUNK), CHUNK), pl.ds(k * kf, kf))
        return remote(act_out.at[part], act.at[part], fs_sem.at[0], fr_sem.at[i, k], above)

    def down(i, k):
        part = (pl.ds(pl.multiple_of(i * CHUNK, CHUNK), CHUNK), pl.ds(k * kw, kw))
        return remote(grad_in.at[part], gath.at[0].at[part], bs_sem.at[0], br_sem.at[i, k], below)

    half = width // 2

    def chunk(i):
        return pl.ds(pl.multiple_of(i * CHUNK, CHUNK), CHUNK)

    per_group = rows // GROUPS

    def gather(part, j, group):
        return remote(
            gath.at[0, part], gath.at[NX - j, part], xs_sem.at[j - 1], xr_sem.at[NX - j - 1, group], at_x(j)
        )

    def n_gather(part, j):
        return remote(
            n_send.at[j - 1, part], n_gath.at[NX - j, part], ns_sem.at[j - 1], nr_sem.at[NX - j - 1], at_x(j)
        )

    def forward(i):
        part = chunk(i)
        square = jnp.zeros((CHUNK, 1), f32)
        for k in range(PIECES_UP):
            cols = pl.ds(k * kf, kf)

            @pl.when(jnp.logical_not(first))
            def _():
                up(i, k).wait_recv()

            a = act[part, cols].astype(f32)
            square = square + jnp.sum(a * a, axis=-1, keepdims=True)

            @pl.when((i == 0) & (before == 0))
            def _():
                for q in range(k * PIECES // PIECES_UP, (k + 1) * PIECES // PIECES_UP):
                    w_load(q).wait()

            @pl.when(jnp.logical_not(last))
            def _():
                b = (act[part, cols].astype(f32) * gains[:, cols]).astype(bf16)
                term = jnp.dot(b, w[cols, :], preferred_element_type=f32)
                if k == 0:
                    acc[...] = term
                else:
                    acc[...] += term

        inv = 1.0 / jnp.sqrt(square / width + eps)
        rinv[part, :] = jnp.broadcast_to(inv, (CHUNK, 128))

        @pl.when(jnp.logical_not(last))
        def _():
            for k in range(PIECES_UP):
                cols = pl.ds(k * kf, kf)
                act_out[part, cols] = (
                    act[part, cols].astype(f32) + acc[:, k * kf : (k + 1) * kf] * inv
                ).astype(bf16)
                up(i, k).start()

        for j in range(NX):
            xj = (x + j) % NX
            for zi in range(nz):
                cols = pl.ds(pl.multiple_of(zi * zw + xj * xw, xw), xw)
                v = (act[part, cols].astype(f32) * inv * gains[:, cols]).astype(bf16)
                if j == 0:
                    n_gath[0, part, zi * xw : (zi + 1) * xw] = v
                else:
                    n_send[j - 1, part, zi * xw : (zi + 1) * xw] = v

        for j in range(1, NX):
            n_gather(part, j).start()

    def backward(i):
        part = chunk(i)
        for k in range(PIECES):
            cols = pl.ds(k * kw, kw)

            @pl.when(jnp.logical_not(last))
            def _():
                down(i, k).wait_recv()

            if k == PIECES - 1:
                for j in (2, 1, 3):
                    gather(part, j, i // (steps // GROUPS)).start()
            term = jnp.dot(gath[0, part, cols], wt[cols, :], preferred_element_type=f32)
            if k == 0:
                acc[...] = term
            else:
                acc[...] += term
        inv = rinv[part, 0:1]
        along = jnp.zeros((CHUNK, 1), f32)
        for k in range(PIECES):
            cols = slice(k * kw, (k + 1) * kw)
            along = along + jnp.sum(
                acc[:, cols] * gains[:, cols] * act[part, cols].astype(f32), axis=-1, keepdims=True
            )
        back = along * (inv * inv * inv) / width
        for k in range(PIECES):
            cols = slice(k * kw, (k + 1) * kw)
            af = act[part, cols].astype(f32)
            dn = acc[:, cols]
            grad_in[part, cols] = (
                gath[0, part, cols].astype(f32) + gains[:, cols] * dn * inv - af * back
            ).astype(bf16)

            @pl.when(jnp.logical_not(first))
            def _():
                down(i, k).start()

        for k in range(PIECES):
            cols = slice(k * kw, (k + 1) * kw)
            v = acc[:, cols] * act[part, cols].astype(f32) * inv
            total = v[0:8]
            for q in range(8, CHUNK, 8):
                total = total + v[q : q + 8]
            gacc[:, cols] += total

    lead = jnp.clip(AHEAD * (2 * (n_section - 1 - s) + 1) // 2, 1, steps)
    side = min(256, width)
    tiles = width // side
    before = jnp.where(s <= 1, 0, tiles * tiles)

    def flip(q, c):
        at = pl.ds(pl.multiple_of(q // tiles * side, side), side)
        to = pl.ds(pl.multiple_of(q % tiles * side, side), side)
        wt[to, at] = w[at, to].T
        return c

    @pl.when(before > 0)
    def _():
        for k in range(PIECES):
            w_load(k).wait()

    lax.fori_loop(0, before, flip, 0)

    far = z >= nz // 2
    z_m = jnp.where(far, nz - 1 - z, z)
    edge = z_m == 0

    def by_role(at_edge, inner):
        return jnp.where(edge, at_edge, inner)

    parts = [by_role(*v) for v in ((3, 2), (2, 3), (1, 0), (0, 1))]

    def z_of(k):
        return jnp.where(far, nz - 1 - k, k)

    most = rows - per_group

    def products(q, tail):
        cols = pl.ds(pl.multiple_of(z_of(parts[q]) * xw, xw), xw)
        tokens = slice(most, rows) if tail else slice(0, most)
        for h in range(2):
            span = slice(h * half, (h + 1) * half)
            total = dw[q, :, span] if tail else None
            for slot in range(NX):
                term = lax.dot_general(
                    n_gath[slot, tokens, cols], gath[slot, tokens, span], (((0,), (0,)), ((), ())),
                    preferred_element_type=f32,
                )
                total = term if total is None else total + term
            dw[q, :, span] = total

    def group_arrived(g):
        for j in range(1, NX):
            gather(pl.ds(g * per_group, per_group), j, g).wait_recv()
            if g == 0:
                n_gather(pl.ds(0, rows), j).wait()

    def most_products():
        for g in range(GROUPS - 1):
            group_arrived(g)
        for q in range(nz):
            products(q, False)

    early = s < n_section // 2

    def step(t, carry):
        @pl.when(t < steps)
        def _():
            forward(t)

        @pl.when(t == lead)
        def _():
            lax.fori_loop(before, tiles * tiles, flip, 0)

        @pl.when((t >= lead) & (t - lead < steps))
        def _():
            backward(t - lead)

        due = jnp.maximum(lead + steps // GROUPS * (GROUPS - 1) - 1, steps - 1) + BEHIND
        due = jnp.minimum(due, 2 * steps - 1)

        @pl.when(early & (t == due))
        def _():
            most_products()

        return carry

    lax.fori_loop(0, 2 * steps, step, 0)

    def gain_x(j):
        return remote(g_send, gx_recv.at[NX - j - 1], gs_sem.at[j - 1], gr_sem.at[NX - j - 1], at_x(j))

    def gain_z(j):
        return remote(
            gz_send, gz_recv.at[nz - j - 1], gs_sem.at[NX + j - 1], gr_sem.at[NX + nz - j - 1], at_z(j)
        )

    gain_core = remote(gc_send, gc_recv, gs_sem.at[NX - 1], gr_sem.at[NX - 1], partner)

    g_send[...] = jnp.sum(gacc[...], axis=0, keepdims=True)
    for j in range(1, NX):
        gain_x(j).start()

    def core_swap(q):
        return remote(core_send.at[q], core_recv.at[q], cs_sem.at[q], cr_sem.at[q], partner)

    def z_send_to(q):
        k = by_role(*((1, 2), (2, 3), (1, 0))[q])
        slot = by_role(*((0, 3), (2, 2), (1, 1))[q])
        to = {"section": s, "dp": (z_of(k) * NX + x) * 2 + core}
        return remote(z_send.at[q], z_recv.at[slot], zs_sem.at[q], zr_sem.at[slot], to)

    def z_arrived(slot):
        return remote(z_send.at[0], z_recv.at[slot], zs_sem.at[0], zr_sem.at[slot], at_z(1))

    mine = pl.ds(pl.multiple_of(core * cw, cw), cw)
    other = pl.ds(pl.multiple_of((1 - core) * cw, cw), cw)

    @pl.when(jnp.logical_not(early))
    def _():
        most_products()

    group_arrived(GROUPS - 1)

    def make(q):
        products(q, True)
        core_send[q] = dw[q, other, :].astype(bf16)
        core_swap(q).start()

    def pass_along(q):
        core_swap(q).wait()
        z_send[q] = (dw[q, mine, :] + core_recv[q].astype(f32)).astype(bf16)

    make(0)
    make(1)
    pass_along(0)
    z_send_to(0).start()
    make(2)
    make(3)
    pass_along(1)
    pass_along(2)

    @pl.when(jnp.logical_not(edge))
    def _():
        z_send_to(2).start()

    for j in range(1, NX):
        gain_x(j).wait()
    total = g_send[...]
    for j in range(1, NX):
        total = total + gx_recv[j - 1]
    gc_send[...] = total
    gain_core.start()
    z_send_to(0).wait_send()

    @pl.when(edge)
    def _():
        z_send_to(1).start()
        z_send_to(2).start()

    @pl.when(jnp.logical_not(edge))
    def _():
        z_arrived(0).wait_recv()
        z_send[1] = (dw[1, mine, :] + core_recv[1].astype(f32) + z_recv[0].astype(f32)).astype(bf16)
        z_send_to(1).start()

    gain_core.wait()
    gz_send[...] = gc_send[...] + gc_recv[...]
    for j in range(1, nz):
        gain_z(j).start()

    core_swap(nz - 1).wait()
    total = dw[nz - 1, mine, :] + core_recv[nz - 1].astype(f32)
    for slot in (1, 2):
        z_arrived(slot).wait_recv()
        total = total + z_recv[slot].astype(f32)
    w_out[...] = total * scale

    @pl.when(jnp.logical_not(edge))
    def _():
        z_arrived(3).wait_recv()
        w_out[...] += z_recv[3].astype(f32) * scale

    total = gz_send[...]
    for j in range(1, nz):
        gain_z(j).wait()
        total = total + gz_recv[nz - j - 1]
    g_out[...] = total * scale

    for q in range(1, nz - 1):
        z_send_to(q).wait_send()
    for j in range(1, NX):
        gather(pl.ds(0, rows), j, 0).wait_send()

    @pl.when(jnp.logical_not(last))
    def _():
        remote(act_out, act, fs_sem.at[0], fr_sem.at[0, 0], above).wait_send()

    @pl.when(jnp.logical_not(first))
    def _():
        remote(grad_in, gath.at[0], bs_sem.at[0], br_sem.at[0, 0], below).wait_send()


def hand_over(*arrays):
    n = len(arrays)

    def copies(*refs):
        sems = refs[2 * n]
        moves = [pltpu.make_async_copy(refs[q], refs[n + q], sems.at[q]) for q in range(n)]
        for move in moves:
            move.start()
        for move in moves:
            move.wait()

    return pl.pallas_call(
        copies,
        out_shape=tuple(jax.ShapeDtypeStruct(a.shape, a.dtype) for a in arrays),
        in_specs=[pl.BlockSpec(memory_space=pl.ANY)] * n,
        out_specs=[pl.BlockSpec(memory_space=pl.ANY)] * n,
        scratch_shapes=[pltpu.SemaphoreType.DMA((n,))],
        name="hand_over",
    )(*arrays)


def on_device(n_section, n_dp, inputs, cotangent, weights, gains):
    micro, tok_rows, width = inputs.shape
    rows = micro * tok_rows
    nz = n_dp // (2 * NX)
    steps = rows // CHUNK
    xw = width // nz // NX
    cw = xw // 2
    scale = 1.0 / math.sqrt(rows * n_dp)
    vmem, dma = pltpu.VMEM, pltpu.SemaphoreType.DMA
    grad_in, w_out, g_out = pl.pallas_call(
        functools.partial(kernel, n_section, n_dp, scale),
        out_shape=(
            vmem((rows, width), bf16),
            vmem((cw, width), f32),
            vmem((1, width), f32),
        ),
        in_specs=[pl.BlockSpec(memory_space=pl.ANY)] * 3 + [pl.BlockSpec(memory_space=vmem)],
        out_specs=[pl.BlockSpec(memory_space=vmem)] * 3,
        scratch_shapes=[
            vmem((width, width), bf16),
            vmem((width, width), bf16),
            vmem((rows, width), bf16),
            vmem((rows, width), bf16),
            vmem((NX, rows, width), bf16),
            vmem((NX - 1, rows, nz * xw), bf16),
            vmem((NX, rows, nz * xw), bf16),
            vmem((rows, 128), f32),
            vmem((CHUNK, width), f32),
            vmem((nz, xw, width), f32),
            vmem((nz, cw, width), bf16),
            vmem((nz, cw, width), bf16),
            vmem((nz - 1, cw, width), bf16),
            vmem((nz, cw, width), bf16),
            vmem((8, width), f32),
            vmem((1, width), f32),
            vmem((NX - 1, 1, width), f32),
            vmem((1, width), f32),
            vmem((1, width), f32),
            vmem((1, width), f32),
            vmem((nz - 1, 1, width), f32),
            dma((2,)),
            dma((PIECES,)),
            dma((1,)),
            dma((steps, PIECES_UP)),
            dma((1,)),
            dma((steps, PIECES)),
            dma((NX - 1,)),
            dma((NX - 1, GROUPS)),
            dma((NX - 1,)),
            dma((NX - 1,)),
            dma((nz,)),
            dma((nz,)),
            dma((nz - 1,)),
            dma((nz,)),
            dma((NX + nz - 1,)),
            dma((NX + nz - 1,)),
        ],
        compiler_params=pltpu.CompilerParams(
            collective_id=0, has_side_effects=True, vmem_limit_bytes=56 * 1024 * 1024
        ),
        name="relay",
    )(inputs.reshape(rows, width), cotangent.reshape(rows, width), weights[0], gains)
    grad_in, w_out, g_out = hand_over(grad_in, w_out, g_out)
    return grad_in.reshape(1, micro, tok_rows, width), w_out[None], g_out


def solution(mesh):
    return jax.shard_map(
        functools.partial(on_device, mesh.shape["section"], mesh.shape["dp"]),
        mesh=mesh,
        in_specs=(
            P(None, "dp", None),
            P(None, "dp", None),
            P("section", None, None),
            P("section", None),
        ),
        out_specs=(P("section", None, "dp", None), P("section", "dp", None), P("section", None)),
        check_vma=False,
    )
```

```python
import functools
import math

import jax
import jax.numpy as jnp
from jax import lax
from jax.experimental import pallas as pl
from jax.experimental.pallas import tpu as pltpu
from jax.sharding import PartitionSpec as P

eps = 1e-05
MESH = pl.DeviceIdType.MESH
NX = 4
CHUNK = 16
PIECES_UP = 2
PIECES = 4
GROUPS = 4
BEHIND = 2
bf16 = jnp.bfloat16
f32 = jnp.float32


def kernel(
    n_section, n_dp, scale,
    inputs, cotangent, weights, gains,
    grad_in, w_out, g_out,
    w, wt, act, act_out, gath, n_send, n_gath, rinv, acc, dw,
    core_send, core_recv, z_send, z_recv, gacc, g_send, gx_recv, gc_send, gc_recv, gz_send, gz_recv,
    load_sem, w_sem, fs_sem, fr_sem, bs_sem, br_sem, xs_sem, xr_sem, ns_sem, nr_sem,
    cs_sem, cr_sem, zs_sem, zr_sem, gs_sem, gr_sem,
):
    rows, width = act.shape
    steps = rows // CHUNK
    kw = width // PIECES
    nz = n_dp // (2 * NX)
    zw = width // nz
    xw = zw // NX
    cw = xw // 2
    s = lax.axis_index("section")
    d = lax.axis_index("dp")
    core = d % 2
    x = (d // 2) % NX
    z = d // (2 * NX)
    first, last = s == 0, s == n_section - 1

    def at_x(j):
        return {"section": s, "dp": (z * NX + (x + j) % NX) * 2 + core}

    def at_z(j):
        return {"section": s, "dp": (((z + j) % nz) * NX + x) * 2 + core}

    partner = {"section": s, "dp": d + 1 - 2 * core}
    above = {"section": (s + 1) % n_section, "dp": d}
    below = {"section": (s + n_section - 1) % n_section, "dp": d}

    def remote(src, dst, send, recv, to):
        return pltpu.make_async_remote_copy(
            src_ref=src, dst_ref=dst, send_sem=send, recv_sem=recv, device_id=to, device_id_type=MESH
        )

    def w_load(k):
        part = pl.ds(k * kw, kw)
        return pltpu.make_async_copy(weights.at[part], w.at[part], w_sem.at[k])

    load_act = pltpu.make_async_copy(inputs, act, load_sem.at[0])
    load_cot = pltpu.make_async_copy(cotangent, gath.at[0], load_sem.at[1])

    @pl.when(first)
    def _():
        load_act.start()

    for k in range(PIECES):
        w_load(k).start()

    @pl.when(last)
    def _():
        load_cot.start()

    gacc[...] = jnp.zeros_like(gacc)

    barrier = pltpu.get_barrier_semaphore()
    peers = [at_x(j) for j in range(1, NX)] + [at_z(j) for j in range(1, nz)] + [partner, above, below]
    for to in peers:
        pl.semaphore_signal(barrier, inc=1, device_id=to, device_id_type=MESH)
    pl.semaphore_wait(barrier, len(peers))

    @pl.when(first)
    def _():
        load_act.wait()

    @pl.when(last)
    def _():
        load_cot.wait()

    kf = width // PIECES_UP

    def up(i, k):
        part = (pl.ds(pl.multiple_of(i * CHUNK, CHUNK), CHUNK), pl.ds(k * kf, kf))
        return remote(act_out.at[part], act.at[part], fs_sem.at[0], fr_sem.at[i, k], above)

    def down(i, k):
        part = (pl.ds(pl.multiple_of(i * CHUNK, CHUNK), CHUNK), pl.ds(k * kw, kw))
        return remote(grad_in.at[part], gath.at[0].at[part], bs_sem.at[0], br_sem.at[i, k], below)

    half = width // 2

    def chunk(i):
        return pl.ds(pl.multiple_of(i * CHUNK, CHUNK), CHUNK)

    per_group = rows // GROUPS

    def gather(part, j, group):
        return remote(
            gath.at[0, part], gath.at[NX - j, part], xs_sem.at[j - 1], xr_sem.at[NX - j - 1, group], at_x(j)
        )

    def n_gather(part, j):
        return remote(
            n_send.at[j - 1, part], n_gath.at[NX - j, part], ns_sem.at[j - 1], nr_sem.at[NX - j - 1], at_x(j)
        )

    def forward(i):
        part = chunk(i)
        square = jnp.zeros((CHUNK, 1), f32)
        for k in range(PIECES_UP):
            cols = pl.ds(k * kf, kf)

            @pl.when(jnp.logical_not(first))
            def _():
                up(i, k).wait_recv()

            a = act[part, cols].astype(f32)
            square = square + jnp.sum(a * a, axis=-1, keepdims=True)

            @pl.when((i == 0) & (before == 0))
            def _():
                for q in range(k * PIECES // PIECES_UP, (k + 1) * PIECES // PIECES_UP):
                    w_load(q).wait()

            @pl.when(jnp.logical_not(last))
            def _():
                b = (act[part, cols].astype(f32) * gains[:, cols]).astype(bf16)
                term = jnp.dot(b, w[cols, :], preferred_element_type=f32)
                if k == 0:
                    acc[...] = term
                else:
                    acc[...] += term

        inv = 1.0 / jnp.sqrt(square / width + eps)
        rinv[part, :] = jnp.broadcast_to(inv, (CHUNK, 128))

        @pl.when(jnp.logical_not(last))
        def _():
            for k in range(PIECES_UP):
                cols = pl.ds(k * kf, kf)
                act_out[part, cols] = (
                    act[part, cols].astype(f32) + acc[:, k * kf : (k + 1) * kf] * inv
                ).astype(bf16)
                up(i, k).start()

        for j in range(NX):
            xj = (x + j) % NX
            for zi in range(nz):
                cols = pl.ds(pl.multiple_of(zi * zw + xj * xw, xw), xw)
                v = (act[part, cols].astype(f32) * inv * gains[:, cols]).astype(bf16)
                if j == 0:
                    n_gath[0, part, zi * xw : (zi + 1) * xw] = v
                else:
                    n_send[j - 1, part, zi * xw : (zi + 1) * xw] = v

        for j in range(1, NX):
            n_gather(part, j).start()

    def backward(i):
        part = chunk(i)
        for k in range(PIECES):
            cols = pl.ds(k * kw, kw)

            @pl.when(jnp.logical_not(last))
            def _():
                down(i, k).wait_recv()

            if k == PIECES - 1:
                for j in (2, 1, 3):
                    gather(part, j, i // (steps // GROUPS)).start()
            term = jnp.dot(gath[0, part, cols], wt[cols, :], preferred_element_type=f32)
            if k == 0:
                acc[...] = term
            else:
                acc[...] += term
        inv = rinv[part, 0:1]
        along = jnp.zeros((CHUNK, 1), f32)
        for k in range(PIECES):
            cols = slice(k * kw, (k + 1) * kw)
            along = along + jnp.sum(
                acc[:, cols] * gains[:, cols] * act[part, cols].astype(f32), axis=-1, keepdims=True
            )
        back = along * (inv * inv * inv) / width
        for k in range(PIECES):
            cols = slice(k * kw, (k + 1) * kw)
            af = act[part, cols].astype(f32)
            dn = acc[:, cols]
            grad_in[part, cols] = (
                gath[0, part, cols].astype(f32) + gains[:, cols] * dn * inv - af * back
            ).astype(bf16)

            @pl.when(jnp.logical_not(first))
            def _():
                down(i, k).start()

        for k in range(PIECES):
            cols = slice(k * kw, (k + 1) * kw)
            v = acc[:, cols] * act[part, cols].astype(f32) * inv
            total = v[0:8]
            for q in range(8, CHUNK, 8):
                total = total + v[q : q + 8]
            gacc[:, cols] += total

    above_me = n_section - 1 - s
    lead = jnp.where(above_me <= 3, jnp.minimum(3 * above_me + above_me // 3, steps), steps)
    side = min(256, width)
    tiles = width // side
    before = jnp.where(s <= 1, 0, tiles * tiles)

    def flip(q, c):
        at = pl.ds(pl.multiple_of(q // tiles * side, side), side)
        to = pl.ds(pl.multiple_of(q % tiles * side, side), side)
        wt[to, at] = w[at, to].T
        return c

    @pl.when(before > 0)
    def _():
        for k in range(PIECES):
            w_load(k).wait()

    lax.fori_loop(0, before, flip, 0)

    far = z >= nz // 2
    z_m = jnp.where(far, nz - 1 - z, z)
    edge = z_m == 0

    def by_role(at_edge, inner):
        return jnp.where(edge, at_edge, inner)

    parts = [by_role(*v) for v in ((3, 2), (2, 3), (1, 0), (0, 1))]

    def z_of(k):
        return jnp.where(far, nz - 1 - k, k)

    most = rows - per_group

    def products(q, tail):
        cols = pl.ds(pl.multiple_of(z_of(parts[q]) * xw, xw), xw)
        tokens = slice(most, rows) if tail else slice(0, most)
        for h in range(2):
            span = slice(h * half, (h + 1) * half)
            total = dw[q, :, span] if tail else None
            for slot in range(NX):
                term = lax.dot_general(
                    n_gath[slot, tokens, cols], gath[slot, tokens, span], (((0,), (0,)), ((), ())),
                    preferred_element_type=f32,
                )
                total = term if total is None else total + term
            dw[q, :, span] = total

    def group_arrived(g):
        for j in range(1, NX):
            gather(pl.ds(g * per_group, per_group), j, g).wait_recv()
            if g == 0:
                n_gather(pl.ds(0, rows), j).wait()

    def most_products():
        for g in range(GROUPS - 1):
            group_arrived(g)
        for q in range(nz):
            products(q, False)

    early = s < n_section // 2

    def step(t, carry):
        @pl.when(t < steps)
        def _():
            forward(t)

        @pl.when(t == lead)
        def _():
            lax.fori_loop(before, tiles * tiles, flip, 0)

        @pl.when((t >= lead) & (t - lead < steps))
        def _():
            backward(t - lead)

        due = jnp.maximum(lead + steps // GROUPS * (GROUPS - 1) - 1, steps - 1) + BEHIND
        due = jnp.minimum(due, 2 * steps - 1)

        @pl.when(early & (t == due))
        def _():
            most_products()

        return carry

    lax.fori_loop(0, 2 * steps, step, 0)

    def gain_x(j):
        return remote(g_send, gx_recv.at[NX - j - 1], gs_sem.at[j - 1], gr_sem.at[NX - j - 1], at_x(j))

    def gain_z(j):
        return remote(
            gz_send, gz_recv.at[nz - j - 1], gs_sem.at[NX + j - 1], gr_sem.at[NX + nz - j - 1], at_z(j)
        )

    gain_core = remote(gc_send, gc_recv, gs_sem.at[NX - 1], gr_sem.at[NX - 1], partner)

    g_send[...] = jnp.sum(gacc[...], axis=0, keepdims=True)
    for j in range(1, NX):
        gain_x(j).start()

    def core_swap(q):
        return remote(core_send.at[q], core_recv.at[q], cs_sem.at[q], cr_sem.at[q], partner)

    def z_send_to(q):
        k = by_role(*((1, 2), (2, 3), (1, 0))[q])
        slot = by_role(*((0, 3), (2, 2), (1, 1))[q])
        to = {"section": s, "dp": (z_of(k) * NX + x) * 2 + core}
        return remote(z_send.at[q], z_recv.at[slot], zs_sem.at[q], zr_sem.at[slot], to)

    def z_arrived(slot):
        return remote(z_send.at[0], z_recv.at[slot], zs_sem.at[0], zr_sem.at[slot], at_z(1))

    mine = pl.ds(pl.multiple_of(core * cw, cw), cw)
    other = pl.ds(pl.multiple_of((1 - core) * cw, cw), cw)

    @pl.when(jnp.logical_not(early))
    def _():
        most_products()

    group_arrived(GROUPS - 1)

    def make(q):
        products(q, True)
        core_send[q] = dw[q, other, :].astype(bf16)
        core_swap(q).start()

    def pass_along(q):
        core_swap(q).wait()
        z_send[q] = (dw[q, mine, :] + core_recv[q].astype(f32)).astype(bf16)

    make(0)
    make(1)
    pass_along(0)
    z_send_to(0).start()
    make(2)
    make(3)
    pass_along(1)
    pass_along(2)

    @pl.when(jnp.logical_not(edge))
    def _():
        z_send_to(2).start()

    for j in range(1, NX):
        gain_x(j).wait()
    total = g_send[...]
    for j in range(1, NX):
        total = total + gx_recv[j - 1]
    gc_send[...] = total
    gain_core.start()
    z_send_to(0).wait_send()

    @pl.when(edge)
    def _():
        z_send_to(1).start()
        z_send_to(2).start()

    @pl.when(jnp.logical_not(edge))
    def _():
        z_arrived(0).wait_recv()
        z_send[1] = (dw[1, mine, :] + core_recv[1].astype(f32) + z_recv[0].astype(f32)).astype(bf16)
        z_send_to(1).start()

    gain_core.wait()
    gz_send[...] = gc_send[...] + gc_recv[...]
    for j in range(1, nz):
        gain_z(j).start()

    core_swap(nz - 1).wait()
    total = dw[nz - 1, mine, :] + core_recv[nz - 1].astype(f32)
    for slot in (1, 2):
        z_arrived(slot).wait_recv()
        total = total + z_recv[slot].astype(f32)
    w_out[...] = total * scale

    @pl.when(jnp.logical_not(edge))
    def _():
        z_arrived(3).wait_recv()
        w_out[...] += z_recv[3].astype(f32) * scale

    total = gz_send[...]
    for j in range(1, nz):
        gain_z(j).wait()
        total = total + gz_recv[nz - j - 1]
    g_out[...] = total * scale

    for q in range(1, nz - 1):
        z_send_to(q).wait_send()
    for j in range(1, NX):
        gather(pl.ds(0, rows), j, 0).wait_send()

    @pl.when(jnp.logical_not(last))
    def _():
        remote(act_out, act, fs_sem.at[0], fr_sem.at[0, 0], above).wait_send()

    @pl.when(jnp.logical_not(first))
    def _():
        remote(grad_in, gath.at[0], bs_sem.at[0], br_sem.at[0, 0], below).wait_send()


def on_device(n_section, n_dp, inputs, cotangent, weights, gains):
    micro, tok_rows, width = inputs.shape
    rows = micro * tok_rows
    nz = n_dp // (2 * NX)
    steps = rows // CHUNK
    xw = width // nz // NX
    cw = xw // 2
    scale = 1.0 / math.sqrt(rows * n_dp)
    vmem, dma = pltpu.VMEM, pltpu.SemaphoreType.DMA
    grad_in, w_out, g_out = pl.pallas_call(
        functools.partial(kernel, n_section, n_dp, scale),
        out_shape=(
            vmem((rows, width), bf16),
            vmem((cw, width), f32),
            vmem((1, width), f32),
        ),
        in_specs=[pl.BlockSpec(memory_space=pl.ANY)] * 3 + [pl.BlockSpec(memory_space=vmem)],
        out_specs=[pl.BlockSpec(memory_space=vmem)] * 3,
        scratch_shapes=[
            vmem((width, width), bf16),
            vmem((width, width), bf16),
            vmem((rows, width), bf16),
            vmem((rows, width), bf16),
            vmem((NX, rows, width), bf16),
            vmem((NX - 1, rows, nz * xw), bf16),
            vmem((NX, rows, nz * xw), bf16),
            vmem((rows, 128), f32),
            vmem((CHUNK, width), f32),
            vmem((nz, xw, width), f32),
            vmem((nz, cw, width), bf16),
            vmem((nz, cw, width), bf16),
            vmem((nz - 1, cw, width), bf16),
            vmem((nz, cw, width), bf16),
            vmem((8, width), f32),
            vmem((1, width), f32),
            vmem((NX - 1, 1, width), f32),
            vmem((1, width), f32),
            vmem((1, width), f32),
            vmem((1, width), f32),
            vmem((nz - 1, 1, width), f32),
            dma((2,)),
            dma((PIECES,)),
            dma((1,)),
            dma((steps, PIECES_UP)),
            dma((1,)),
            dma((steps, PIECES)),
            dma((NX - 1,)),
            dma((NX - 1, GROUPS)),
            dma((NX - 1,)),
            dma((NX - 1,)),
            dma((nz,)),
            dma((nz,)),
            dma((nz - 1,)),
            dma((nz,)),
            dma((NX + nz - 1,)),
            dma((NX + nz - 1,)),
        ],
        compiler_params=pltpu.CompilerParams(
            collective_id=0, has_side_effects=True, vmem_limit_bytes=56 * 1024 * 1024
        ),
        name="relay",
    )(inputs.reshape(rows, width), cotangent.reshape(rows, width), weights[0], gains)
    return grad_in.reshape(1, micro, tok_rows, width), w_out[None], g_out


def solution(mesh):
    return jax.shard_map(
        functools.partial(on_device, mesh.shape["section"], mesh.shape["dp"]),
        mesh=mesh,
        in_specs=(
            P(None, "dp", None),
            P(None, "dp", None),
            P("section", None, None),
            P("section", None),
        ),
        out_specs=(P("section", None, "dp", None), P("section", "dp", None), P("section", None)),
        check_vma=False,
    )
```

```python
import functools
import math

import jax
import jax.numpy as jnp
from jax import lax
from jax.experimental import pallas as pl
from jax.experimental.pallas import tpu as pltpu
from jax.sharding import PartitionSpec as P

eps = 1e-05
MESH = pl.DeviceIdType.MESH
NX = 4
CHUNK = 16
PIECES_UP = 4
PIECES = 4
GROUPS = 4
BEHIND = 2
bf16 = jnp.bfloat16
f32 = jnp.float32


def kernel(
    n_section, n_dp, scale,
    inputs, cotangent, weights, gains,
    grad_in, w_out, g_out,
    w, wt, act, act_out, gath, n_send, n_gath, rinv, acc, dw,
    core_send, core_recv, z_send, z_recv, gacc, g_send, gx_recv, gc_send, gc_recv, gz_send, gz_recv,
    load_sem, w_sem, fs_sem, fr_sem, bs_sem, br_sem, xs_sem, xr_sem, ns_sem, nr_sem,
    cs_sem, cr_sem, zs_sem, zr_sem, gs_sem, gr_sem,
):
    rows, width = act.shape
    steps = rows // CHUNK
    kw = width // PIECES
    nz = n_dp // (2 * NX)
    zw = width // nz
    xw = zw // NX
    cw = xw // 2
    s = lax.axis_index("section")
    d = lax.axis_index("dp")
    core = d % 2
    x = (d // 2) % NX
    z = d // (2 * NX)
    first, last = s == 0, s == n_section - 1

    def at_x(j):
        return {"section": s, "dp": (z * NX + (x + j) % NX) * 2 + core}

    def at_z(j):
        return {"section": s, "dp": (((z + j) % nz) * NX + x) * 2 + core}

    partner = {"section": s, "dp": d + 1 - 2 * core}
    above = {"section": (s + 1) % n_section, "dp": d}
    below = {"section": (s + n_section - 1) % n_section, "dp": d}

    def remote(src, dst, send, recv, to):
        return pltpu.make_async_remote_copy(
            src_ref=src, dst_ref=dst, send_sem=send, recv_sem=recv, device_id=to, device_id_type=MESH
        )

    def w_load(k):
        part = pl.ds(k * kw, kw)
        return pltpu.make_async_copy(weights.at[part], w.at[part], w_sem.at[k])

    load_act = pltpu.make_async_copy(inputs, act, load_sem.at[0])
    load_cot = pltpu.make_async_copy(cotangent, gath.at[0], load_sem.at[1])

    @pl.when(first)
    def _():
        load_act.start()

    for k in range(PIECES):
        w_load(k).start()

    @pl.when(last)
    def _():
        load_cot.start()

    gacc[...] = jnp.zeros_like(gacc)

    barrier = pltpu.get_barrier_semaphore()
    peers = [at_x(j) for j in range(1, NX)] + [at_z(j) for j in range(1, nz)] + [partner, above, below]
    for to in peers:
        pl.semaphore_signal(barrier, inc=1, device_id=to, device_id_type=MESH)
    pl.semaphore_wait(barrier, len(peers))

    @pl.when(first)
    def _():
        load_act.wait()

    @pl.when(last)
    def _():
        load_cot.wait()

    kf = width // PIECES_UP

    def up(i, k):
        part = (pl.ds(pl.multiple_of(i * CHUNK, CHUNK), CHUNK), pl.ds(k * kf, kf))
        return remote(act_out.at[part], act.at[part], fs_sem.at[0], fr_sem.at[i, k], above)

    def down(i, k):
        part = (pl.ds(pl.multiple_of(i * CHUNK, CHUNK), CHUNK), pl.ds(k * kw, kw))
        return remote(grad_in.at[part], gath.at[0].at[part], bs_sem.at[0], br_sem.at[i, k], below)

    half = width // 2

    def chunk(i):
        return pl.ds(pl.multiple_of(i * CHUNK, CHUNK), CHUNK)

    per_group = rows // GROUPS

    def gather(part, j, group):
        return remote(
            gath.at[0, part], gath.at[NX - j, part], xs_sem.at[j - 1], xr_sem.at[NX - j - 1, group], at_x(j)
        )

    def n_gather(part, j):
        return remote(
            n_send.at[j - 1, part], n_gath.at[NX - j, part], ns_sem.at[j - 1], nr_sem.at[NX - j - 1], at_x(j)
        )

    def forward(i):
        part = chunk(i)
        square = jnp.zeros((CHUNK, 1), f32)
        for k in range(PIECES_UP):
            cols = pl.ds(k * kf, kf)

            @pl.when(jnp.logical_not(first))
            def _():
                up(i, k).wait_recv()

            a = act[part, cols].astype(f32)
            square = square + jnp.sum(a * a, axis=-1, keepdims=True)

            @pl.when((i == 0) & (before == 0))
            def _():
                for q in range(k * PIECES // PIECES_UP, (k + 1) * PIECES // PIECES_UP):
                    w_load(q).wait()

            @pl.when(jnp.logical_not(last))
            def _():
                b = (act[part, cols].astype(f32) * gains[:, cols]).astype(bf16)
                term = jnp.dot(b, w[cols, :], preferred_element_type=f32)
                if k == 0:
                    acc[...] = term
                else:
                    acc[...] += term

        inv = 1.0 / jnp.sqrt(square / width + eps)
        rinv[part, :] = jnp.broadcast_to(inv, (CHUNK, 128))

        @pl.when(jnp.logical_not(last))
        def _():
            for k in range(PIECES_UP):
                cols = pl.ds(k * kf, kf)
                act_out[part, cols] = (
                    act[part, cols].astype(f32) + acc[:, k * kf : (k + 1) * kf] * inv
                ).astype(bf16)
                up(i, k).start()

        for j in range(NX):
            xj = (x + j) % NX
            for zi in range(nz):
                cols = pl.ds(pl.multiple_of(zi * zw + xj * xw, xw), xw)
                v = (act[part, cols].astype(f32) * inv * gains[:, cols]).astype(bf16)
                if j == 0:
                    n_gath[0, part, zi * xw : (zi + 1) * xw] = v
                else:
                    n_send[j - 1, part, zi * xw : (zi + 1) * xw] = v

        for j in range(1, NX):
            n_gather(part, j).start()

    def backward(i):
        part = chunk(i)
        for k in range(PIECES):
            cols = pl.ds(k * kw, kw)

            @pl.when(jnp.logical_not(last))
            def _():
                down(i, k).wait_recv()

            if k == PIECES - 1:
                for j in (2, 1, 3):
                    gather(part, j, i // (steps // GROUPS)).start()
            term = jnp.dot(gath[0, part, cols], wt[cols, :], preferred_element_type=f32)
            if k == 0:
                acc[...] = term
            else:
                acc[...] += term
        inv = rinv[part, 0:1]
        along = jnp.zeros((CHUNK, 1), f32)
        for k in range(PIECES):
            cols = slice(k * kw, (k + 1) * kw)
            along = along + jnp.sum(
                acc[:, cols] * gains[:, cols] * act[part, cols].astype(f32), axis=-1, keepdims=True
            )
        back = along * (inv * inv * inv) / width
        for k in range(PIECES):
            cols = slice(k * kw, (k + 1) * kw)
            af = act[part, cols].astype(f32)
            dn = acc[:, cols]
            grad_in[part, cols] = (
                gath[0, part, cols].astype(f32) + gains[:, cols] * dn * inv - af * back
            ).astype(bf16)

            @pl.when(jnp.logical_not(first))
            def _():
                down(i, k).start()

        for k in range(PIECES):
            cols = slice(k * kw, (k + 1) * kw)
            v = acc[:, cols] * act[part, cols].astype(f32) * inv
            total = v[0:8]
            for q in range(8, CHUNK, 8):
                total = total + v[q : q + 8]
            gacc[:, cols] += total

    above_me = n_section - 1 - s
    lead = jnp.where(above_me <= 3, jnp.minimum(3 * above_me + above_me // 3, steps), steps)
    side = min(256, width)
    tiles = width // side
    before = jnp.where(s <= 1, 0, tiles * tiles)

    def flip(q, c):
        at = pl.ds(pl.multiple_of(q // tiles * side, side), side)
        to = pl.ds(pl.multiple_of(q % tiles * side, side), side)
        wt[to, at] = w[at, to].T
        return c

    @pl.when(before > 0)
    def _():
        for k in range(PIECES):
            w_load(k).wait()

    lax.fori_loop(0, before, flip, 0)

    far = z >= nz // 2
    z_m = jnp.where(far, nz - 1 - z, z)
    edge = z_m == 0

    def by_role(at_edge, inner):
        return jnp.where(edge, at_edge, inner)

    parts = [by_role(*v) for v in ((3, 2), (2, 3), (1, 0), (0, 1))]

    def z_of(k):
        return jnp.where(far, nz - 1 - k, k)

    most = rows - per_group

    def products(q, tail):
        cols = pl.ds(pl.multiple_of(z_of(parts[q]) * xw, xw), xw)
        tokens = slice(most, rows) if tail else slice(0, most)
        for h in range(2):
            span = slice(h * half, (h + 1) * half)
            total = dw[q, :, span] if tail else None
            for slot in range(NX):
                term = lax.dot_general(
                    n_gath[slot, tokens, cols], gath[slot, tokens, span], (((0,), (0,)), ((), ())),
                    preferred_element_type=f32,
                )
                total = term if total is None else total + term
            dw[q, :, span] = total

    def group_arrived(g):
        for j in range(1, NX):
            gather(pl.ds(g * per_group, per_group), j, g).wait_recv()
            if g == 0:
                n_gather(pl.ds(0, rows), j).wait()

    def most_products():
        for g in range(GROUPS - 1):
            group_arrived(g)
        for q in range(nz):
            products(q, False)

    early = s < n_section // 2

    def step(t, carry):
        @pl.when(t < steps)
        def _():
            forward(t)

        @pl.when(t == lead)
        def _():
            lax.fori_loop(before, tiles * tiles, flip, 0)

        @pl.when((t >= lead) & (t - lead < steps))
        def _():
            backward(t - lead)

        due = jnp.maximum(lead + steps // GROUPS * (GROUPS - 1) - 1, steps - 1) + BEHIND
        due = jnp.minimum(due, 2 * steps - 1)

        @pl.when(early & (t == due))
        def _():
            most_products()

        return carry

    lax.fori_loop(0, 2 * steps, step, 0)

    def gain_x(j):
        return remote(g_send, gx_recv.at[NX - j - 1], gs_sem.at[j - 1], gr_sem.at[NX - j - 1], at_x(j))

    def gain_z(j):
        return remote(
            gz_send, gz_recv.at[nz - j - 1], gs_sem.at[NX + j - 1], gr_sem.at[NX + nz - j - 1], at_z(j)
        )

    gain_core = remote(gc_send, gc_recv, gs_sem.at[NX - 1], gr_sem.at[NX - 1], partner)

    g_send[...] = jnp.sum(gacc[...], axis=0, keepdims=True)
    for j in range(1, NX):
        gain_x(j).start()

    def core_swap(q):
        return remote(core_send.at[q], core_recv.at[q], cs_sem.at[q], cr_sem.at[q], partner)

    def z_send_to(q):
        k = by_role(*((1, 2), (2, 3), (1, 0))[q])
        slot = by_role(*((0, 3), (2, 2), (1, 1))[q])
        to = {"section": s, "dp": (z_of(k) * NX + x) * 2 + core}
        return remote(z_send.at[q], z_recv.at[slot], zs_sem.at[q], zr_sem.at[slot], to)

    def z_arrived(slot):
        return remote(z_send.at[0], z_recv.at[slot], zs_sem.at[0], zr_sem.at[slot], at_z(1))

    mine = pl.ds(pl.multiple_of(core * cw, cw), cw)
    other = pl.ds(pl.multiple_of((1 - core) * cw, cw), cw)

    @pl.when(jnp.logical_not(early))
    def _():
        most_products()

    group_arrived(GROUPS - 1)

    def make(q):
        products(q, True)
        core_send[q] = dw[q, other, :].astype(bf16)
        core_swap(q).start()

    def pass_along(q):
        core_swap(q).wait()
        z_send[q] = (dw[q, mine, :] + core_recv[q].astype(f32)).astype(bf16)

    make(0)
    make(1)
    pass_along(0)
    z_send_to(0).start()
    make(2)
    make(3)
    pass_along(1)
    pass_along(2)

    @pl.when(jnp.logical_not(edge))
    def _():
        z_send_to(2).start()

    for j in range(1, NX):
        gain_x(j).wait()
    total = g_send[...]
    for j in range(1, NX):
        total = total + gx_recv[j - 1]
    gc_send[...] = total
    gain_core.start()
    z_send_to(0).wait_send()

    @pl.when(edge)
    def _():
        z_send_to(1).start()
        z_send_to(2).start()

    @pl.when(jnp.logical_not(edge))
    def _():
        z_arrived(0).wait_recv()
        z_send[1] = (dw[1, mine, :] + core_recv[1].astype(f32) + z_recv[0].astype(f32)).astype(bf16)
        z_send_to(1).start()

    gain_core.wait()
    gz_send[...] = gc_send[...] + gc_recv[...]
    for j in range(1, nz):
        gain_z(j).start()

    core_swap(nz - 1).wait()
    total = dw[nz - 1, mine, :] + core_recv[nz - 1].astype(f32)
    for slot in (1, 2):
        z_arrived(slot).wait_recv()
        total = total + z_recv[slot].astype(f32)
    w_out[...] = total * scale

    @pl.when(jnp.logical_not(edge))
    def _():
        z_arrived(3).wait_recv()
        w_out[...] += z_recv[3].astype(f32) * scale

    total = gz_send[...]
    for j in range(1, nz):
        gain_z(j).wait()
        total = total + gz_recv[nz - j - 1]
    g_out[...] = total * scale

    for q in range(1, nz - 1):
        z_send_to(q).wait_send()
    for j in range(1, NX):
        gather(pl.ds(0, rows), j, 0).wait_send()

    @pl.when(jnp.logical_not(last))
    def _():
        remote(act_out, act, fs_sem.at[0], fr_sem.at[0, 0], above).wait_send()

    @pl.when(jnp.logical_not(first))
    def _():
        remote(grad_in, gath.at[0], bs_sem.at[0], br_sem.at[0, 0], below).wait_send()


def on_device(n_section, n_dp, inputs, cotangent, weights, gains):
    micro, tok_rows, width = inputs.shape
    rows = micro * tok_rows
    nz = n_dp // (2 * NX)
    steps = rows // CHUNK
    xw = width // nz // NX
    cw = xw // 2
    scale = 1.0 / math.sqrt(rows * n_dp)
    vmem, dma = pltpu.VMEM, pltpu.SemaphoreType.DMA
    grad_in, w_out, g_out = pl.pallas_call(
        functools.partial(kernel, n_section, n_dp, scale),
        out_shape=(
            vmem((rows, width), bf16),
            vmem((cw, width), f32),
            vmem((1, width), f32),
        ),
        in_specs=[pl.BlockSpec(memory_space=pl.ANY)] * 3 + [pl.BlockSpec(memory_space=vmem)],
        out_specs=[pl.BlockSpec(memory_space=vmem)] * 3,
        scratch_shapes=[
            vmem((width, width), bf16),
            vmem((width, width), bf16),
            vmem((rows, width), bf16),
            vmem((rows, width), bf16),
            vmem((NX, rows, width), bf16),
            vmem((NX - 1, rows, nz * xw), bf16),
            vmem((NX, rows, nz * xw), bf16),
            vmem((rows, 128), f32),
            vmem((CHUNK, width), f32),
            vmem((nz, xw, width), f32),
            vmem((nz, cw, width), bf16),
            vmem((nz, cw, width), bf16),
            vmem((nz - 1, cw, width), bf16),
            vmem((nz, cw, width), bf16),
            vmem((8, width), f32),
            vmem((1, width), f32),
            vmem((NX - 1, 1, width), f32),
            vmem((1, width), f32),
            vmem((1, width), f32),
            vmem((1, width), f32),
            vmem((nz - 1, 1, width), f32),
            dma((2,)),
            dma((PIECES,)),
            dma((1,)),
            dma((steps, PIECES_UP)),
            dma((1,)),
            dma((steps, PIECES)),
            dma((NX - 1,)),
            dma((NX - 1, GROUPS)),
            dma((NX - 1,)),
            dma((NX - 1,)),
            dma((nz,)),
            dma((nz,)),
            dma((nz - 1,)),
            dma((nz,)),
            dma((NX + nz - 1,)),
            dma((NX + nz - 1,)),
        ],
        compiler_params=pltpu.CompilerParams(
            collective_id=0, has_side_effects=True, vmem_limit_bytes=56 * 1024 * 1024
        ),
        name="relay",
    )(inputs.reshape(rows, width), cotangent.reshape(rows, width), weights[0], gains)
    return grad_in.reshape(1, micro, tok_rows, width), w_out[None], g_out


def solution(mesh):
    return jax.shard_map(
        functools.partial(on_device, mesh.shape["section"], mesh.shape["dp"]),
        mesh=mesh,
        in_specs=(
            P(None, "dp", None),
            P(None, "dp", None),
            P("section", None, None),
            P("section", None),
        ),
        out_specs=(P("section", None, "dp", None), P("section", "dp", None), P("section", None)),
        check_vma=False,
    )
```
